32 devices in a mesh: grp: 2 (over x), suf: 4 (over y, core), head: 4 (over z).
Axes of the slice: x: 2, y: 2, z: 4, core: 2. Of those that a mesh axis runs over, the one named last changes fastest.
Arguments:
- prefix_x: bfloat16 [1024, 8192], P(('grp', 'suf'), 'head'), parts along dimension 0, may hold values from -6 to 6
- prefix_b: bfloat16 [1024, 1024], P(('grp', 'suf'), 'head'), parts along dimension 0, may hold values from -6 to 6
- prefix_c: bfloat16 [1024, 1024], P(('grp', 'suf'), 'head'), parts along dimension 0, may hold values from -6 to 6
- prefix_dt: float32 [128, 1024], P('head', ('grp', 'suf')), parts along dimension 1, may hold values from -3 to 3
- prefix_grad: bfloat16 [1024, 8192], P(('grp', 'suf'), 'head'), parts along dimension 0, may hold values from -0.59765625 to 0.59765625
- suffix_x: bfloat16 [8, 128, 8192], P(('grp', 'suf'), None, 'head'), parts along dimension 0, may hold values from -6 to 6
- suffix_b: bfloat16 [8, 128, 1024], P(('grp', 'suf'), None, 'head'), parts along dimension 0, may hold values from -6 to 6
- suffix_c: bfloat16 [8, 128, 1024], P(('grp', 'suf'), None, 'head'), parts along dimension 0, may hold values from -6 to 6
- suffix_dt: float32 [128, 8, 128], P('head', ('grp', 'suf')), parts along dimension 1, may hold values from -3 to 3
- suffix_grad: bfloat16 [8, 128, 8192], P(('grp', 'suf'), None, 'head'), parts along dimension 0, may hold values from -0.59765625 to 0.59765625
- lengths: int32 [8], P(('grp', 'suf')), parts along dimension 0, may hold values from 1 to 128, 384 in all
- loss_mask: int32 [8, 128], P(('grp', 'suf')), parts along dimension 0, may hold values 0 or 1
- advantage: float32 [8], P(('grp', 'suf')), parts along dimension 0, may hold values from -3 to 3
- conv_x: bfloat16 [4, 8192], P(None, 'head'), may hold values from -3 to 3
- conv_b: bfloat16 [4, 1024], P(None, 'head'), may hold values from -3 to 3
- conv_c: bfloat16 [4, 1024], P(None, 'head'), may hold values from -3 to 3
- decay_rate: float32 [128], P('head'), may hold values from 7.8125e-05 to 0.05
- dt_bias: float32 [128], P('head'), may hold values from -1 to 0.5
- skip: float32 [128], P('head'), may hold values from 0.5 to 1.5
Outputs:
- prefix_dx: bfloat16 [1024, 8192], P(('grp', 'suf'), 'head'), parts along dimension 0
- prefix_db: bfloat16 [1024, 1024], P(('grp', 'suf'), 'head'), parts along dimension 0
- prefix_dc: bfloat16 [1024, 1024], P(('grp', 'suf'), 'head'), parts along dimension 0
- prefix_ddt: float32 [128, 1024], P('head', ('grp', 'suf')), parts along dimension 1
- suffix_dx: bfloat16 [8, 128, 8192], P(('grp', 'suf'), None, 'head'), parts along dimension 0
- suffix_db: bfloat16 [8, 128, 1024], P(('grp', 'suf'), None, 'head'), parts along dimension 0
- suffix_dc: bfloat16 [8, 128, 1024], P(('grp', 'suf'), None, 'head'), parts along dimension 0
- suffix_ddt: float32 [128, 8, 128], P('head', ('grp', 'suf')), parts along dimension 1
The draws below stay inside these ranges and needn't reach their ends.
There are 2 independent parts, one for each index of `grp`. The reference program is written for one: setup_inputs(seed, part) draws one part's arguments, and reference() takes and returns one part's arrays. A program takes and returns all parts, laid end to end along the dimension named above; an argument that names none is the same for every part. Nothing has to cross between parts.
Inputs may be any that keep to these rules, and one draw needn't show every extreme that they name: `lengths`: some suffix has exactly 128 tokens.
All inputs are finite; a program needn't handle non-finite values. No bound on the sum of `lengths` or of `loss_mask` on one device may be relied on, other than what follows from the above.
Results may differ from the reference program's by a relative error of at most 0.001.
Values may be sent and summed in bfloat16 or wider, within the bound.
A program may use at most 128 MiB of HBM per device.

```python
import math
import jax
import jax.numpy as jnp
import numpy as np
from jax import lax

H = 128
HD = 64
N = 128
G = 8
KW = 4
Q = 128
LEN = 128
PREFIX = 512
SUFFIXES = 4


def place_ends(values, key, least, largest):
    shape = values.shape
    index_at = [jax.random.randint(jax.random.fold_in(key, axis), (), 0, shape[axis]) for axis in range(len(shape))]
    values = values.at[tuple(index_at)].set(least)
    longest = shape.index(max(shape))
    index_at[longest] = (index_at[longest] + 1) % shape[longest]
    return values.at[tuple(index_at)].set(largest)


def block_scale(key, dims, cuts, low, top_value):
    loudness, own = 1.0, jax.random.fold_in(key, 6)
    for axis_at, shards_of in cuts:
        steps = jnp.exp(jax.random.uniform(jax.random.fold_in(own, axis_at), (shards_of,), jnp.float32, low / len(cuts), top_value / len(cuts)))
        loudness = loudness * jnp.repeat(steps, dims[axis_at] // shards_of).reshape([-1 if axis == axis_at else 1 for axis in range(len(dims))])
    return loudness


def length_profile(number_of, total, bound, slope):
    loads = [(1 << 20) // math.isqrt(standing ** slope) + 1 for standing in range(2, number_of + 1)]
    rest, counts = total - bound - (number_of - 1), [1] * (number_of - 1)
    while rest > 0:
        candidates = [i for i in range(number_of - 1) if counts[i] < bound]
        pool, budget = sum([loads[i] for i in candidates]), rest
        for i in candidates:
            addition = min(bound - counts[i], max(1, budget * loads[i] // pool), rest)
            counts[i] = counts[i] + addition
            rest = rest - addition
    return np.array([bound] + counts)


def ragged_sizes(key, number_of, total, reach, lean):
    if number_of == 2:
        one = jax.random.randint(key, (), max(1, total - reach), min(reach, total - 1) + 1)
        return jnp.stack([one, total - one])
    tallies = jnp.asarray(length_profile(number_of, total, reach, lean), jnp.int32)
    pairs = (number_of - 1) // 2
    source_of, sink = tallies[1:1 + 2 * pairs:2], tallies[2:2 + 2 * pairs:2]
    room = jnp.minimum(source_of - 1, reach - sink)
    shifted = jax.random.randint(jax.random.fold_in(key, 1), (pairs,), 0, 1 << 20) % (room + 1)
    tallies = tallies.at[1:1 + 2 * pairs:2].set(source_of - shifted).at[2:2 + 2 * pairs:2].set(sink + shifted)
    return tallies[jax.random.permutation(jax.random.fold_in(key, 2), number_of)]


def noise(stream_key, extent, width, reach, shards=(), kind=jnp.bfloat16):
    array = jax.random.normal(stream_key, extent, jnp.float32) * width
    if len(shards) > 0:
        array = block_scale(stream_key, extent, shards, -0.22, 0.18) * array
    return jnp.clip(array, min=-reach, max=reach).astype(kind)


def setup_inputs(seed: int = 0, part: int = 0) -> dict:
    key_list = jax.random.split(jax.random.key(seed), 20)
    part_splits = jax.random.split(jax.random.fold_in(key_list[19], part), 20)
    prefix_x = noise(part_splits[0], (PREFIX, H * HD), 1.0, 6.0, ((0, 4), (1, 4)))
    prefix_b = noise(part_splits[1], (PREFIX, G * N), 1.0, 6.0, ((0, 4), (1, 4)))
    prefix_c = noise(part_splits[2], (PREFIX, G * N), 1.0, 6.0, ((0, 4), (1, 4)))
    prefix_dt = noise(part_splits[3], (H, PREFIX), 0.5, 3.0, ((0, 4), (1, 4)), jnp.float32)
    prefix_grad = noise(part_splits[4], (PREFIX, H * HD), 0.1, 0.59765625, ((0, 4), (1, 4)))
    suffix_x = noise(part_splits[5], (SUFFIXES, LEN, H * HD), 1.0, 6.0, ((0, 4), (2, 4)))
    suffix_b = noise(part_splits[6], (SUFFIXES, LEN, G * N), 1.0, 6.0, ((0, 4), (2, 4)))
    suffix_c = noise(part_splits[7], (SUFFIXES, LEN, G * N), 1.0, 6.0, ((0, 4), (2, 4)))
    suffix_dt = noise(part_splits[8], (H, SUFFIXES, LEN), 0.5, 3.0, ((0, 4), (1, 4)), jnp.float32)
    suffix_grad = noise(part_splits[9], (SUFFIXES, LEN, H * HD), 0.1, 0.59765625, ((0, 4), (2, 4)))
    lengths = ragged_sizes(part_splits[10], SUFFIXES, 3 * SUFFIXES * LEN // 4, LEN, 1).astype(jnp.int32)
    loss_mask = place_ends((jax.random.randint(part_splits[11], (SUFFIXES, LEN), 0, 4) < 3).astype(jnp.int32), jax.random.fold_in(part_splits[11], 1), 0, 1)
    advantage = noise(part_splits[12], (SUFFIXES,), 1.0, 3.0, ((0, 4),), jnp.float32)
    conv_x = noise(key_list[13], (KW, H * HD), KW ** -0.5, 3.0, ((1, 4),))
    conv_b = noise(key_list[14], (KW, G * N), KW ** -0.5, 3.0, ((1, 4),))
    conv_c = noise(key_list[15], (KW, G * N), KW ** -0.5, 3.0, ((1, 4),))
    decay_rate = jnp.clip(jnp.exp(math.log(0.05) - 6.461468 * jax.random.uniform(key_list[16], (H,), jnp.float32) ** block_scale(key_list[16], (H,), ((0, 4),), -0.2, 0.2)), 7.812499825377017e-05, 0.05)
    dt_bias = jnp.clip(-1.0 + 1.5 * jax.random.uniform(key_list[17], (H,), jnp.float32) ** block_scale(key_list[17], (H,), ((0, 4),), -0.2, 0.2), -1.0, 0.5)
    skip = jnp.clip(0.5 + 1.0 * jax.random.uniform(key_list[18], (H,), jnp.float32) ** block_scale(key_list[18], (H,), ((0, 4),), -0.2, 0.2), 0.5, 1.5)
    return dict(prefix_x=prefix_x, prefix_b=prefix_b, prefix_c=prefix_c, prefix_dt=prefix_dt, prefix_grad=prefix_grad, suffix_x=suffix_x, suffix_b=suffix_b, suffix_c=suffix_c, suffix_dt=suffix_dt, suffix_grad=suffix_grad, lengths=lengths, loss_mask=loss_mask, advantage=advantage, conv_x=conv_x, conv_b=conv_b, conv_c=conv_c, decay_rate=decay_rate, dt_bias=dt_bias, skip=skip)


EXACT_DOT = lax.Precision.HIGHEST

def causal_conv(values, context, taps):
    padded = jnp.concatenate([context, values], axis=0)
    num_tokens = values.shape[0]
    result = padded[0:num_tokens] * taps[0].astype(jnp.float32)
    for tap_index in range(1, taps.shape[0]):
        result = result + padded[tap_index:tap_index + num_tokens] * taps[tap_index].astype(jnp.float32)
    return jax.nn.silu(result)

def run_scan(x_act, b_act, c_act, step_dt, decay_rates, skip_gain, start_state):
    tokens = x_act.shape[0]
    num_heads = x_act.shape[1]
    num_groups = b_act.shape[1]
    per_group = num_heads // num_groups
    blocks = tokens // Q
    x_blocks = x_act.reshape(blocks, Q, num_groups, per_group, HD)
    b_blocks = b_act.reshape(blocks, Q, num_groups, N)
    c_blocks = c_act.reshape(blocks, Q, num_groups, N)
    log_decay = (-step_dt * decay_rates[:, None]).reshape(num_groups, per_group, blocks, Q).transpose(2, 0, 1, 3)
    dt_blocks = step_dt.reshape(num_groups, per_group, blocks, Q).transpose(2, 0, 1, 3)
    lower_tri = jnp.arange(Q)[:, None] >= jnp.arange(Q)[None, :]
    skip_shaped = skip_gain.reshape(num_groups, per_group)[:, :, None]

    def advance(current, pieces):
        x_block, b_block, c_block, log_block, dt_block = pieces
        cumulative = jnp.cumsum(log_block, axis=-1)
        log_gaps = cumulative[..., :, None] - cumulative[..., None, :]
        within = jnp.where(lower_tri, jnp.exp(jnp.where(lower_tri, log_gaps, 0.0)), 0.0)
        scores = jnp.einsum('tgn,sgn->gts', c_block, b_block, precision=EXACT_DOT)
        mixing = scores[:, None] * within * dt_block[:, :, None, :]
        inner_out = jnp.einsum('gkts,sgkp->tgkp', mixing, x_block, precision=EXACT_DOT)
        carried = jnp.einsum('tgn,gkpn->tgkp', c_block, current, precision=EXACT_DOT)
        carried = carried * jnp.exp(cumulative).transpose(2, 0, 1)[..., None]
        output = inner_out + carried + skip_shaped * x_block
        weights = jnp.exp(cumulative[..., -1:] - cumulative) * dt_block
        updated = current * jnp.exp(cumulative[..., -1])[..., None, None]
        updated = updated + jnp.einsum('gks,sgkp,sgn->gkpn', weights, x_block, b_block, precision=EXACT_DOT)
        return (updated, output)
    last_state, outputs = lax.scan(jax.checkpoint(advance), start_state.reshape(num_groups, per_group, HD, N), (x_blocks, b_blocks, c_blocks, log_decay, dt_blocks))
    return (outputs.reshape(tokens, num_heads * HD), last_state.reshape(num_heads, HD, N))

def block_forward(x_feat, b_feat, c_feat, dt_raw, left_x, left_b, left_c, start_state, params):
    conv_x, conv_b, conv_c, decay_rates, dt_offset, skip_gain = params
    num_heads = decay_rates.shape[0]
    num_groups = conv_b.shape[1] // N
    x_act = causal_conv(x_feat, left_x, conv_x).reshape(-1, num_heads, HD)
    b_act = causal_conv(b_feat, left_b, conv_b).reshape(-1, num_groups, N)
    c_act = causal_conv(c_feat, left_c, conv_c).reshape(-1, num_groups, N)
    step_dt = jax.nn.softplus(dt_raw + dt_offset[:, None])
    return run_scan(x_act, b_act, c_act, step_dt, decay_rates, skip_gain, start_state)

def reference(prefix_x, prefix_b, prefix_c, prefix_dt, prefix_grad, suffix_x, suffix_b, suffix_c, suffix_dt, suffix_grad, lengths, loss_mask, advantage, conv_x, conv_b, conv_c, decay_rate, dt_bias, skip):
    margin = KW - 1
    params = (conv_x, conv_b, conv_c, decay_rate, dt_bias, skip)

    def forward(prompt_x, prompt_b, prompt_c, prompt_dt, samp_x, samp_b, samp_c, samp_dt):
        zero_x = jnp.zeros((margin, prompt_x.shape[1]), jnp.float32)
        zero_b = jnp.zeros((margin, prompt_b.shape[1]), jnp.float32)
        zero_state = jnp.zeros((H, HD, N), jnp.float32)
        prompt_out, prompt_end = block_forward(prompt_x, prompt_b, prompt_c, prompt_dt, zero_x, zero_b, zero_b, zero_state, params)

        def one_suffix(items):
            x_one, b_one, c_one, dt_one = items
            out_one, unused_end = block_forward(x_one, b_one, c_one, dt_one, prompt_x[-margin:], prompt_b[-margin:], prompt_c[-margin:], prompt_end, params)
            return out_one
        suffix_out = lax.map(one_suffix, (samp_x, samp_b, samp_c, jnp.transpose(samp_dt, (1, 0, 2))))
        return (prompt_out, suffix_out)
    primals = (prefix_x.astype(jnp.float32), prefix_b.astype(jnp.float32), prefix_c.astype(jnp.float32), prefix_dt, suffix_x.astype(jnp.float32), suffix_b.astype(jnp.float32), suffix_c.astype(jnp.float32), suffix_dt)
    unused_out, pullback = jax.vjp(forward, primals[0], primals[1], primals[2], primals[3], primals[4], primals[5], primals[6], primals[7])
    positions = jnp.arange(LEN)[None, :]
    valid = (positions < lengths[:, None]).astype(jnp.float32)
    weight = advantage[:, None] * loss_mask.astype(jnp.float32) * valid
    suffix_cot = weight[:, :, None] * suffix_grad.astype(jnp.float32)
    grads = pullback((prefix_grad.astype(jnp.float32), suffix_cot))
    return (grads[0].astype(jnp.bfloat16), grads[1].astype(jnp.bfloat16), grads[2].astype(jnp.bfloat16), grads[3], grads[4].astype(jnp.bfloat16), grads[5].astype(jnp.bfloat16), grads[6].astype(jnp.bfloat16), grads[7])
```

```python
import functools

import jax
import jax.numpy as jnp
from jax import lax
from jax.experimental import pallas as pl
from jax.experimental.pallas import tpu as pltpu
from jax.sharding import PartitionSpec as P

HD = 64
N = 128
KW = 4
Q = 128
F32 = jnp.float32
BF16 = jnp.bfloat16
EXACT = lax.Precision.HIGHEST
MESH = pl.DeviceIdType.MESH
NN = (((1,), (0,)), ((), ()))
NT = (((1,), (1,)), ((), ()))


def mm(a, b, dims=NN):
    return lax.dot_general(a, b, dims, preferred_element_type=F32)


def split(a):
    hi = a.astype(BF16)
    return hi, (a - hi.astype(F32)).astype(BF16)


def mm3(a, b, dims=NN):
    ah, al = a
    bh, bl = b
    axis = dims[0][1][0]
    return mm(
        jnp.concatenate([ah, ah, al], axis=1), jnp.concatenate([bh, bl, bh], axis=axis), dims
    )


def conv_pre(halo, u, taps):
    w = jnp.concatenate([halo.astype(F32), u.astype(F32)], axis=0)
    taps = taps.astype(F32)
    out = w[5 : 5 + Q] * taps[0:1]
    for k in range(1, KW):
        out = out + w[5 + k : 5 + k + Q] * taps[k : k + 1]
    return out


def silu(v):
    return v * jax.nn.sigmoid(v)


def conv_back(dact, pre, taps):
    taps = taps.astype(F32)
    sig = jax.nn.sigmoid(pre)
    dpre = dact * (sig * (1.0 + pre * (1.0 - sig)))
    zero = jnp.zeros((8, dpre.shape[1]), F32)
    ext = jnp.concatenate([zero, dpre, zero], axis=0)
    du = ext[11 : 11 + Q] * taps[0:1]
    left = ext[8:16] * taps[0:1]
    for k in range(1, KW):
        du = du + ext[11 - k : 11 - k + Q] * taps[k : k + 1]
        left = left + ext[8 - k : 16 - k] * taps[k : k + 1]
    return du, left


def softplus(v):
    return jnp.maximum(v, 0.0) + jnp.log1p(jnp.exp(-jnp.abs(v)))


def tri(transposed=False):
    row = lax.broadcasted_iota(jnp.int32, (Q, Q), 0)
    col = lax.broadcasted_iota(jnp.int32, (Q, Q), 1)
    return (row >= col) if transposed else (row <= col)


def expander(heads):
    row = lax.broadcasted_iota(jnp.int32, (heads, heads * HD), 0)
    col = lax.broadcasted_iota(jnp.int32, (heads, heads * HD), 1)
    return ((col >= row * HD) & (col < (row + 1) * HD)).astype(F32)


def decays(dt_ref, bias_ref, rate_ref):
    raw = dt_ref[...] + bias_ref[...]
    step = softplus(raw)
    cum = lax.dot_general(
        -step * rate_ref[...], tri().astype(F32), NN, precision=EXACT, preferred_element_type=F32
    )
    return raw, step, cum


def widen(rows, spread):
    return lax.dot_general(rows.T, spread, NN, precision=EXACT, preferred_element_type=F32)


def row_weight(len_ref, adv_ref, mask_ref):
    at = lax.broadcasted_iota(jnp.int32, (1, Q), 1)
    inside = (at < len_ref[0]).astype(F32)
    return adv_ref[0] * mask_ref[...].astype(F32) * inside


def states_kernel(
    len_ref, adv_ref, mask_ref,
    px, pb, pc, pdt, pg, phx, phb, phc,
    sx, sb, sc, sdt, sg, shx, shb, shc,
    tx, tb, tc, rate, bias, skip,
    own_ref, adj_ref, suf_ref, dec_ref,
):
    heads = pdt.shape[0]
    spread = expander(heads)
    raw, step, cum = decays(pdt, bias, rate)
    last = cum[:, Q - 1 : Q]
    push = widen(jnp.exp(last - cum) * step, spread)
    pull = jnp.exp(cum)
    pull_wide = widen(pull, spread)
    dec_ref[...] = jnp.broadcast_to(pull_wide[Q - 1 : Q], dec_ref.shape)
    b_t = split(silu(conv_pre(phb[...], pb[...], tb[...])).T)
    c_t = split(silu(conv_pre(phc[...], pc[...], tc[...])).T)
    x_act = silu(conv_pre(phx[...], px[...], tx[...]))
    own_ref[...] = mm3(b_t, split(x_act * push))
    adj_ref[...] = mm3(c_t, split(pg[...].astype(F32) * pull_wide))
    s_raw, s_step, s_cum = decays(sdt, bias, rate)
    weight = row_weight(len_ref, adv_ref, mask_ref)
    s_pull = widen(jnp.exp(s_cum) * weight, spread)
    sc_t = split(silu(conv_pre(shc[...], sc[...], tc[...])).T)
    suf_ref[...] = mm3(sc_t, split(sg[...].astype(F32) * s_pull))


def within(x_ref, b_ref, c_ref, dt_ref, g_ref, hx, hb, hc, tx, tb, tc, rate, bias, weight,
           dx_out, db_out, dc_out, r_out):
    heads = dt_ref.shape[0]
    raw, step, cum = decays(dt_ref, bias, rate)
    cum_col = cum.T
    step_col = step.T
    b_act = split(silu(conv_pre(hb[...], b_ref[...], tb[...])))
    c_act = split(silu(conv_pre(hc[...], c_ref[...], tc[...])))
    bc = mm3(b_act, c_act, NT)
    keep = tri()
    lane = lax.broadcasted_iota(jnp.int32, (Q, 2 * HD), 1)
    total = jnp.zeros((Q, Q), F32)
    width = heads * HD
    chunk = min(width, 2 * HD)
    for at in range(0, width, chunk):
        cols = slice(at, at + chunk)
        x_act = silu(conv_pre(hx[:, cols], x_ref[:, cols], tx[:, cols]))
        grad = g_ref[:, cols]
        xh, xl = split(x_act)
        twice = jnp.concatenate([grad, grad], axis=1)
        left, right = [], []
        for k in range(chunk // HD):
            h = at // HD + k
            if chunk == HD:
                xhm, xlm, gm = xh, xl, grad
            else:
                mine = (lane >= k * HD) & (lane < (k + 1) * HD)
                zero = jnp.zeros((), BF16)
                xhm = jnp.where(mine, xh, zero)
                xlm = jnp.where(mine, xl, zero)
                gm = jnp.where(mine, grad, zero)
            gap = jnp.where(keep, cum[h : h + 1] - cum_col[:, h : h + 1], -1e30)
            att = jnp.exp(gap) * step_col[:, h : h + 1]
            if weight is not None:
                att = att * weight
            dm = mm(jnp.concatenate([xhm, xlm], axis=1), twice, NT)
            q = dm * att
            total = total + q
            r_out[h : h + 1] = jnp.sum(q * bc, axis=0, keepdims=True)
            mh, ml = split(att * bc)
            left += [mh, ml]
            right += [gm, gm]
        dx_out[:, cols] = mm(jnp.concatenate(left, axis=1), jnp.concatenate(right, axis=0))
    db_out[...] = mm3(split(total), c_act)
    dc_out[...] = mm3(split(total.T), b_act)


def within_kernel(
    len_ref, adv_ref, mask_ref,
    px, pb, pc, pdt, pg, phx, phb, phc,
    sx, sb, sc, sdt, sg, shx, shb, shc,
    tx, tb, tc, rate, bias, skip,
    p_dx, p_db, p_dc, p_r, s_dx, s_db, s_dc, s_r,
):
    within(px, pb, pc, pdt, pg, phx, phb, phc, tx, tb, tc, rate, bias, None, p_dx, p_db, p_dc, p_r)
    weight = row_weight(len_ref, adv_ref, mask_ref)
    within(sx, sb, sc, sdt, sg, shx, shb, shc, tx, tb, tc, rate, bias, weight, s_dx, s_db, s_dc, s_r)


def per_head(spread, value):
    hi, lo = split(value)
    e = spread.astype(BF16)
    return mm(e, hi, NT) + mm(e, lo, NT)


def carried(x_ref, b_ref, c_ref, dt_ref, g_ref, hx, hb, hc, tx, tb, tc, rate, bias, skip, weight,
            start, adjoint, in_dx, in_db, in_dc, in_r, dx, db, dc, ddt, lx, lb, lc, tails):
    heads = dt_ref.shape[0]
    spread = expander(heads)
    raw, step, cum = decays(dt_ref, bias, rate)
    pull = jnp.exp(cum)
    if weight is not None:
        pull = pull * weight
    pull_wide = widen(pull, spread)
    gain = skip[...] if weight is None else skip[...] * weight
    gain_wide = widen(jnp.broadcast_to(gain, (heads, Q)), spread)
    b_pre = conv_pre(hb[...], b_ref[...], tb[...])
    c_pre = conv_pre(hc[...], c_ref[...], tc[...])
    x_pre = conv_pre(hx[...], x_ref[...], tx[...])
    x_act = silu(x_pre)
    grad = g_ref[...].astype(F32)
    c_act = split(silu(c_pre))
    s_split = split(start[...])
    pulled = grad * pull_wide
    across = per_head(spread, pulled * mm3(c_act, s_split))
    dc_act = in_dc[...] + mm3(split(pulled), s_split, NT)
    db_act = in_db[...]
    dx_in = in_dx[...]
    col_sum = per_head(spread, x_act * dx_in)
    end = jnp.zeros((heads, 1), F32)
    if adjoint is not None:
        last = cum[:, Q - 1 : Q]
        push = widen(jnp.exp(last - cum) * step, spread)
        b_act = split(silu(b_pre))
        a_split = split(adjoint[...])
        moved = push * mm3(b_act, a_split)
        dx_in = dx_in + moved
        v = per_head(spread, x_act * moved)
        col_sum = col_sum + v
        db_act = db_act + mm3(split(x_act * push), a_split, NT)
        both = jnp.sum(per_head(spread, start[...] * adjoint[...]), axis=1, keepdims=True)
        end = jnp.sum(v, axis=1, keepdims=True) + jnp.exp(last) * both
    change = in_r[...] + across - col_sum
    dlog = end + lax.dot_general(
        change, tri(True).astype(F32), NN, precision=EXACT, preferred_element_type=F32
    )
    ddt[...] = (col_sum / step - rate[...] * dlog) * jax.nn.sigmoid(raw)
    for dact, pre, taps, out, left, tail in (
        (dx_in + gain_wide * grad, x_pre, tx, dx, lx, 0),
        (db_act, b_pre, tb, db, lb, 1),
        (dc_act, c_pre, tc, dc, lc, 2),
    ):
        du, dleft = conv_back(dact, pre, taps[...])
        out[...] = du.astype(BF16)
        left[...] = dleft
        if tails is not None:
            tails[tail][...] = du[Q - 8 :]


def carried_kernel(
    len_ref, adv_ref, mask_ref,
    px, pb, pc, pdt, pg, phx, phb, phc,
    sx, sb, sc, sdt, sg, shx, shb, shc,
    tx, tb, tc, rate, bias, skip,
    p_start, p_adj, s_start,
    p_idx, p_idb, p_idc, p_r, s_idx, s_idb, s_idc, s_r,
    p_dx, p_db, p_dc, p_ddt, s_dx, s_db, s_dc, s_ddt,
    plx, plb, plc, slx, slb, slc, ptx, ptb, ptc,
):
    carried(px, pb, pc, pdt, pg, phx, phb, phc, tx, tb, tc, rate, bias, skip, None,
            p_start, p_adj, p_idx, p_idb, p_idc, p_r, p_dx, p_db, p_dc, p_ddt,
            plx, plb, plc, (ptx, ptb, ptc))
    weight = row_weight(len_ref, adv_ref, mask_ref)
    carried(sx, sb, sc, sdt, sg, shx, shb, shc, tx, tb, tc, rate, bias, skip, weight,
            s_start, None, s_idx, s_idb, s_idc, s_r, s_dx, s_db, s_dc, s_ddt,
            slx, slb, slc, None)


def gather_kernel(ways, x_ref, out_ref, send, recv, own):
    me = lax.axis_index("suf")
    barrier = pltpu.get_barrier_semaphore()
    for d in range(1, ways):
        pl.semaphore_signal(
            barrier, inc=1, device_id={"suf": lax.rem(me + d, ways)}, device_id_type=MESH
        )
    pl.semaphore_wait(barrier, ways - 1)
    copies = []
    for d in range(1, ways):
        copies.append(
            pltpu.make_async_remote_copy(
                src_ref=x_ref,
                dst_ref=out_ref.at[d],
                send_sem=send.at[d],
                recv_sem=recv.at[d],
                device_id={"suf": lax.rem(me + d, ways)},
                device_id_type=MESH,
            )
        )
        copies[-1].start()
    mine = pltpu.make_async_copy(x_ref, out_ref.at[0], own)
    mine.start()
    mine.wait()
    for copy in copies:
        copy.wait()


def gather_small(block, ways, ident):
    if ways == 1:
        return block[None]
    return pl.pallas_call(
        functools.partial(gather_kernel, ways),
        out_shape=jax.ShapeDtypeStruct((ways,) + block.shape, block.dtype),
        in_specs=[pl.BlockSpec(memory_space=pltpu.VMEM)],
        out_specs=pl.BlockSpec(memory_space=pltpu.VMEM),
        scratch_shapes=[
            pltpu.SemaphoreType.DMA((ways,)),
            pltpu.SemaphoreType.DMA((ways,)),
            pltpu.SemaphoreType.DMA,
        ],
        compiler_params=pltpu.CompilerParams(collective_id=ident, has_side_effects=True),
    )(block)


def exchange(parts, bit, ways):
    route = [(i, i ^ bit) for i in range(ways)]
    return [lax.ppermute(part, "suf", route) for part in parts]


def combine(own, adj, suf, dec, ways):
    me = lax.axis_index("suf")
    start = jnp.zeros_like(own)
    before = jnp.ones_like(dec)
    tail = jnp.zeros_like(adj)
    after = jnp.ones_like(dec)
    bit = 1
    while bit < ways:
        upper = (me & bit) != 0
        final = bit * 2 == ways
        if final:
            second = jnp.where(upper, adj + dec * suf, suf)
            own_, second_, dec_ = exchange((own, second, dec), bit, ways)
            start = jnp.where(upper, before * own_ + start, start)
            end = jnp.where(upper, dec * own_ + own, dec_ * own + own_)
            total = suf + second_
            tail = jnp.where(
                upper, tail + after * total, tail + after * (second_ + dec_ * suf)
            )
            return start, end, tail
        own_, adj_, suf_, dec_ = exchange((own, adj, suf, dec), bit, ways)
        start = jnp.where(upper, before * own_ + start, start)
        before = jnp.where(upper, before * dec_, before)
        tail = jnp.where(upper, tail, tail + after * adj_)
        after = jnp.where(upper, after, after * dec_)
        own = jnp.where(upper, dec * own_ + own, dec_ * own + own_)
        adj = jnp.where(upper, adj_ + dec_ * adj, adj + dec * adj_)
        suf = suf + suf_
        dec = dec * dec_
        bit *= 2
    return start, own, tail + after * suf


def shards(
    prefix_x, prefix_b, prefix_c, prefix_dt, prefix_grad,
    suffix_x, suffix_b, suffix_c, suffix_dt, suffix_grad,
    lengths, loss_mask, advantage, conv_x, conv_b, conv_c, decay_rate, dt_bias, skip,
):
    ways = lax.axis_size("suf")
    me = lax.axis_index("suf")
    heads = decay_rate.shape[0]
    groups = conv_b.shape[1] // N
    per = heads // groups
    wide = per * HD
    full = heads * HD
    nb = groups * N
    margin = KW - 1

    tails = jnp.concatenate([prefix_x[-16:], prefix_b[-16:], prefix_c[-16:]], axis=1)
    gathered = gather_small(tails, ways, 0)[:, 8:]
    left = jnp.where(me == 0, jnp.zeros_like(gathered[0]), gathered[1 % ways])
    context = lax.dynamic_index_in_dim(gathered, lax.rem(me + 1, ways), 0, False)

    def cut(block):
        return block[:, :full], block[:, full : full + nb], block[:, full + nb :]

    sm = pl.BlockSpec(memory_space=pltpu.SMEM)
    sx = pl.BlockSpec((Q, wide), lambda g: (0, g))
    sb = pl.BlockSpec((Q, N), lambda g: (0, g))
    sdt = pl.BlockSpec((per, Q), lambda g: (g, 0))
    hx = pl.BlockSpec((8, wide), lambda g: (0, g))
    hb = pl.BlockSpec((8, N), lambda g: (0, g))
    kx = pl.BlockSpec((KW, wide), lambda g: (0, g))
    kb = pl.BlockSpec((KW, N), lambda g: (0, g))
    ph = pl.BlockSpec((per, 1), lambda g: (g, 0))
    half = [sx, sb, sb, sdt, sx, hx, hb, hb]
    base_specs = (
        [sm, sm, pl.BlockSpec((1, Q), lambda g: (0, 0))] + half + half + [kx, kb, kb, ph, ph, ph]
    )
    base = (
        (lengths, advantage, loss_mask)
        + (prefix_x, prefix_b, prefix_c, prefix_dt, prefix_grad)
        + cut(left)
        + (suffix_x[0], suffix_b[0], suffix_c[0], suffix_dt[:, 0], suffix_grad[0])
        + cut(context)
        + (conv_x, conv_b, conv_c, decay_rate[:, None], dt_bias[:, None], skip[:, None])
    )

    def shape(rows, columns, kind=F32):
        return jax.ShapeDtypeStruct((rows, columns), kind)

    params = pltpu.CompilerParams(vmem_limit_bytes=48 * 1024 * 1024)
    state_shape = shape(N, full)
    own, adj, suf, dec = pl.pallas_call(
        states_kernel,
        grid=(groups,),
        in_specs=base_specs,
        out_specs=[sx, sx, sx, hx],
        out_shape=[state_shape] * 3 + [shape(8, full)],
        compiler_params=params,
        name="states",
    )(*base)

    inner_specs = [sx, sb, sb, sdt]
    inner_shape = [shape(Q, full), shape(Q, nb), shape(Q, nb), shape(heads, Q)]
    inner = pl.pallas_call(
        within_kernel,
        grid=(groups,),
        in_specs=base_specs,
        out_specs=inner_specs * 2,
        out_shape=inner_shape * 2,
        compiler_params=params,
        cost_estimate=pl.CostEstimate(
            flops=heads * 2 * 12 * Q * Q * Q, bytes_accessed=6 << 20, transcendentals=heads * Q * Q
        ),
        name="within",
    )(*base)

    start, end, adjoint = combine(own, adj, suf, dec[:1], ways)

    out_specs = [sx, sb, sb, sdt] * 2 + [hx, hb, hb] * 3
    out_shape = [shape(Q, full, BF16), shape(Q, nb, BF16), shape(Q, nb, BF16), shape(heads, Q)] * 2
    out_shape += [shape(8, full), shape(8, nb), shape(8, nb)] * 3
    outs = pl.pallas_call(
        carried_kernel,
        grid=(groups,),
        in_specs=base_specs + [sx, sx, sx] + inner_specs * 2,
        out_specs=out_specs,
        out_shape=out_shape,
        compiler_params=params,
        name="carried",
    )(*base, start, adjoint, end, *inner)

    lefts = jnp.concatenate(outs[8:11], axis=1)[:margin]
    sufs = jnp.concatenate(outs[11:14], axis=1)[:margin]
    pad = jnp.zeros((8 - margin, lefts.shape[1]), F32)
    message = jnp.concatenate([lefts, pad, sufs, pad], axis=0)
    got = gather_small(message, ways, 1)
    extra = jnp.where(
        me == ways - 1, jnp.sum(got[:, 8 : 8 + margin], axis=0), got[ways - 1, :margin]
    )
    finished = []
    for at, add in enumerate(cut(extra)):
        tail = (outs[14 + at][-margin:] + add).astype(BF16)
        finished.append(outs[at].at[-margin:].set(tail))
    return (
        *finished,
        outs[3],
        outs[4][None],
        outs[5][None],
        outs[6][None],
        outs[7][:, None],
    )


def solution(mesh):
    rows = P(("grp", "suf"), "head")
    deep = P(("grp", "suf"), None, "head")
    flat = P("head", ("grp", "suf"))
    flat3 = P("head", ("grp", "suf"), None)
    one = P(("grp", "suf"))
    return jax.shard_map(
        shards,
        mesh=mesh,
        in_specs=(
            rows, rows, rows, flat, rows,
            deep, deep, deep, flat3, deep,
            one, P(("grp", "suf"), None), one,
            P(None, "head"), P(None, "head"), P(None, "head"),
            P("head"), P("head"), P("head"),
        ),
        out_specs=(rows, rows, rows, flat, deep, deep, deep, flat3),
        check_vma=False,
    )
```

```python
import functools

import jax
import jax.numpy as jnp
from jax import lax
from jax.experimental import pallas as pl
from jax.experimental.pallas import tpu as pltpu
from jax.sharding import PartitionSpec as P

HD = 64
N = 128
KW = 4
Q = 128
F32 = jnp.float32
BF16 = jnp.bfloat16
EXACT = lax.Precision.HIGHEST
MESH = pl.DeviceIdType.MESH
NN = (((1,), (0,)), ((), ()))
NT = (((1,), (1,)), ((), ()))


def mm(a, b, dims=NN):
    return lax.dot_general(a, b, dims, preferred_element_type=F32)


def split(a):
    hi = a.astype(BF16)
    return hi, (a - hi.astype(F32)).astype(BF16)


def mm3(a, b, dims=NN):
    ah, al = a
    bh, bl = b
    axis = dims[0][1][0]
    return mm(
        jnp.concatenate([ah, ah, al], axis=1), jnp.concatenate([bh, bl, bh], axis=axis), dims
    )


def conv_pre(halo, u, taps):
    w = jnp.concatenate([halo.astype(F32)[8:], u.astype(F32)], axis=0)
    taps = taps.astype(F32)
    out = w[5 : 5 + Q] * taps[0:1]
    for k in range(1, KW):
        out = out + w[5 + k : 5 + k + Q] * taps[k : k + 1]
    return out


def silu(v):
    return v * jax.nn.sigmoid(v)


def conv_back(dact, pre, taps):
    taps = taps.astype(F32)
    sig = jax.nn.sigmoid(pre)
    dpre = dact * (sig * (1.0 + pre * (1.0 - sig)))
    zero = jnp.zeros((8, dpre.shape[1]), F32)
    ext = jnp.concatenate([zero, dpre, zero], axis=0)
    du = ext[11 : 11 + Q] * taps[0:1]
    left = ext[8:16] * taps[0:1]
    for k in range(1, KW):
        du = du + ext[11 - k : 11 - k + Q] * taps[k : k + 1]
        left = left + ext[8 - k : 16 - k] * taps[k : k + 1]
    return du, left


def softplus(v):
    return jnp.maximum(v, 0.0) + jnp.log1p(jnp.exp(-jnp.abs(v)))


def tri(transposed=False):
    row = lax.broadcasted_iota(jnp.int32, (Q, Q), 0)
    col = lax.broadcasted_iota(jnp.int32, (Q, Q), 1)
    return (row >= col) if transposed else (row <= col)


def expander(heads):
    row = lax.broadcasted_iota(jnp.int32, (heads, heads * HD), 0)
    col = lax.broadcasted_iota(jnp.int32, (heads, heads * HD), 1)
    return ((col >= row * HD) & (col < (row + 1) * HD)).astype(F32)


def decays(dt_ref, bias_ref, rate_ref):
    raw = dt_ref[...] + bias_ref[...]
    step = softplus(raw)
    cum = lax.dot_general(
        -step * rate_ref[...], tri().astype(F32), NN, precision=EXACT, preferred_element_type=F32
    )
    return raw, step, cum


def widen(rows, spread):
    v = rows.T
    hi, rest = split(v)
    lo = (v - hi.astype(F32) - rest.astype(F32)).astype(BF16)
    e = spread.astype(BF16)
    return mm(jnp.concatenate([hi, rest, lo], axis=1), jnp.concatenate([e, e, e], axis=0))


def row_weight(len_ref, adv_ref, mask_ref):
    at = lax.broadcasted_iota(jnp.int32, (1, Q), 1)
    inside = (at < len_ref[0]).astype(F32)
    return adv_ref[0] * mask_ref[...].astype(F32) * inside


def states_kernel(
    len_ref, adv_ref, mask_ref,
    px, pb, pc, pdt, pg, phx, phb, phc,
    sx, sb, sc, sdt, sg, shx, shb, shc,
    tx, tb, tc, rate, bias, skip,
    own_ref, adj_ref, suf_ref, dec_ref,
):
    heads = pdt.shape[0]
    spread = expander(heads)
    raw, step, cum = decays(pdt, bias, rate)
    last = cum[:, Q - 1 : Q]
    push = widen(jnp.exp(last - cum) * step, spread)
    pull = jnp.exp(cum)
    pull_wide = widen(pull, spread)
    dec_ref[...] = jnp.broadcast_to(pull_wide[Q - 1 : Q], dec_ref.shape)
    b_t = split(silu(conv_pre(phb[...], pb[...], tb[...])).T)
    c_t = split(silu(conv_pre(phc[...], pc[...], tc[...])).T)
    x_act = silu(conv_pre(phx[...], px[...], tx[...]))
    own_ref[...] = mm3(b_t, split(x_act * push))
    adj_ref[...] = mm3(c_t, split(pg[...].astype(F32) * pull_wide))
    s_raw, s_step, s_cum = decays(sdt, bias, rate)
    weight = row_weight(len_ref, adv_ref, mask_ref)
    s_pull = widen(jnp.exp(s_cum) * weight, spread)
    sc_t = split(silu(conv_pre(shc[...], sc[...], tc[...])).T)
    suf_ref[...] = mm3(sc_t, split(sg[...].astype(F32) * s_pull))


def within(x_ref, b_ref, c_ref, dt_ref, g_ref, hx, hb, hc, tx, tb, tc, rate, bias, weight,
           dx_out, db_out, dc_out, r_out):
    heads = dt_ref.shape[0]
    raw, step, cum = decays(dt_ref, bias, rate)
    cum_col = cum.T
    step_col = step.T
    b_act = split(silu(conv_pre(hb[...], b_ref[...], tb[...])))
    c_act = split(silu(conv_pre(hc[...], c_ref[...], tc[...])))
    bc = mm3(b_act, c_act, NT)
    keep = tri()
    lane = lax.broadcasted_iota(jnp.int32, (Q, 2 * HD), 1)
    total = jnp.zeros((Q, Q), F32)
    width = heads * HD
    chunk = min(width, 2 * HD)
    for at in range(0, width, chunk):
        cols = slice(at, at + chunk)
        x_act = silu(conv_pre(hx[:, cols], x_ref[:, cols], tx[:, cols]))
        grad = g_ref[:, cols]
        xh, xl = split(x_act)
        twice = jnp.concatenate([grad, grad], axis=1)
        left, right = [], []
        for k in range(chunk // HD):
            h = at // HD + k
            if chunk == HD:
                xhm, xlm, gm = xh, xl, grad
            else:
                mine = (lane >= k * HD) & (lane < (k + 1) * HD)
                zero = jnp.zeros((), BF16)
                xhm = jnp.where(mine, xh, zero)
                xlm = jnp.where(mine, xl, zero)
                gm = jnp.where(mine, grad, zero)
            gap = jnp.where(keep, cum[h : h + 1] - cum_col[:, h : h + 1], -1e30)
            att = jnp.exp(gap) * step_col[:, h : h + 1]
            if weight is not None:
                att = att * weight
            dm = mm(jnp.concatenate([xhm, xlm], axis=1), twice, NT)
            q = dm * att
            total = total + q
            r_out[h : h + 1] = jnp.sum(q * bc, axis=0, keepdims=True)
            mh, ml = split(att * bc)
            left += [mh, ml]
            right += [gm, gm]
        dx_out[:, cols] = mm(jnp.concatenate(left, axis=1), jnp.concatenate(right, axis=0))
    db_out[...] = mm3(split(total), c_act)
    dc_out[...] = mm3(split(total.T), b_act)


def within_kernel(
    len_ref, adv_ref, mask_ref,
    px, pb, pc, pdt, pg, phx, phb, phc,
    sx, sb, sc, sdt, sg, shx, shb, shc,
    tx, tb, tc, rate, bias, skip,
    p_dx, p_db, p_dc, p_r, s_dx, s_db, s_dc, s_r,
):
    within(px, pb, pc, pdt, pg, phx, phb, phc, tx, tb, tc, rate, bias, None, p_dx, p_db, p_dc, p_r)
    weight = row_weight(len_ref, adv_ref, mask_ref)
    within(sx, sb, sc, sdt, sg, shx, shb, shc, tx, tb, tc, rate, bias, weight, s_dx, s_db, s_dc, s_r)


def per_head(value, gather):
    hi, lo = split(value)
    return mm(jnp.concatenate([hi, lo], axis=1), gather)


def carried(x_ref, b_ref, c_ref, dt_ref, g_ref, hx, hb, hc, tx, tb, tc, rate, bias, skip, weight,
            state, in_dx, in_db, in_dc, in_r, dx, db, dc, ddt, lefts, tails):
    heads = dt_ref.shape[0]
    spread = expander(heads)
    raw, step, cum = decays(dt_ref, bias, rate)
    pull = jnp.exp(cum)
    if weight is not None:
        pull = pull * weight
    gain = skip[...] if weight is None else skip[...] * weight
    gain = jnp.broadcast_to(gain, (heads, Q))
    last = cum[:, Q - 1 : Q]
    push = jnp.exp(last - cum) * step
    b_pre = conv_pre(hb[...], b_ref[...], tb[...])
    c_pre = conv_pre(hc[...], c_ref[...], tc[...])
    b_act = split(silu(b_pre))
    c_act = split(silu(c_pre))
    dc_act = in_dc[...]
    db_act = in_db[...]
    width = heads * HD
    chunk = min(width, 256)
    across = jnp.zeros((Q, heads), F32)
    col_sum = jnp.zeros((Q, heads), F32)
    v = jnp.zeros((Q, heads), F32)
    both = jnp.zeros((8, heads), F32)
    first = 0 if weight is None else 3
    head_of = lax.broadcasted_iota(jnp.int32, (chunk, heads), 1) * HD
    lane_of = lax.broadcasted_iota(jnp.int32, (chunk, heads), 0)

    def finish(dact, pre, taps, out, left, tail, cols):
        du, dleft = conv_back(dact, pre, taps)
        out[:, cols] = du.astype(BF16)
        left[first : first + 3, cols] = dleft[:3]
        if tail is not None:
            tail[:, cols] = du[Q - 8 :]

    for at in range(0, width, chunk):
        cols = slice(at, at + chunk)
        inside = (lane_of + at >= head_of) & (lane_of + at < head_of + HD)
        gather = inside.astype(BF16)
        gather = jnp.concatenate([gather, gather], axis=0)
        part = spread[:, cols]
        grad = g_ref[:, cols].astype(F32)
        x_pre = conv_pre(hx[:, cols], x_ref[:, cols], tx[:, cols])
        x_act = silu(x_pre)
        start, adjoint = state(cols)
        s_split = split(start)
        pulled = grad * widen(pull, part)
        across = across + per_head(pulled * mm3(c_act, s_split), gather)
        dc_act = dc_act + mm3(split(pulled), s_split, NT)
        dx_in = in_dx[:, cols]
        if adjoint is not None:
            push_wide = widen(push, part)
            a_split = split(adjoint)
            moved = push_wide * mm3(b_act, a_split)
            dx_in = dx_in + moved
            v = v + per_head(x_act * moved, gather)
            db_act = db_act + mm3(split(x_act * push_wide), a_split, NT)
            product = jnp.sum(start * adjoint, axis=0, keepdims=True)
            both = both + per_head(jnp.broadcast_to(product, (8, chunk)), gather)
        col_sum = col_sum + per_head(x_act * dx_in, gather)
        dx_act = dx_in + widen(gain, part) * grad
        finish(dx_act, x_pre, tx[:, cols], dx, lefts[0], tails and tails[0], cols)
    whole = slice(0, N)
    finish(db_act, b_pre, tb[...], db, lefts[1], tails and tails[1], whole)
    finish(dc_act, c_pre, tc[...], dc, lefts[2], tails and tails[2], whole)
    end = jnp.sum(v, axis=0, keepdims=True).T
    if weight is None:
        end = end + jnp.exp(last) * both.T[:, :1]
    cols_t = col_sum.T
    change = in_r[...] + across.T - cols_t
    dlog = end + lax.dot_general(
        change, tri(True).astype(F32), NN, precision=EXACT, preferred_element_type=F32
    )
    ddt[...] = (cols_t / step - rate[...] * dlog) * jax.nn.sigmoid(raw)


def carried_kernel(
    len_ref, adv_ref, mask_ref,
    px, pb, pc, pdt, pg, phx, phb, phc,
    sx, sb, sc, sdt, sg, shx, shb, shc,
    tx, tb, tc, rate, bias, skip,
    start, own, tail, suf, own_q, sec_q, rows,
    p_idx, p_idb, p_idc, p_r, s_idx, s_idb, s_idc, s_r,
    p_dx, p_db, p_dc, p_ddt, s_dx, s_db, s_dc, s_ddt,
    lx, lb, lc, ptx, ptb, ptc,
):
    for left in (lx, lb, lc):
        left[...] = jnp.zeros_like(left)

    def prompt_state(cols):
        other = own_q[:, cols].astype(F32)
        second = sec_q[:, cols].astype(F32)
        begin = start[:, cols] + rows[0:1, cols] * other
        adjoint = tail[:, cols] + rows[3:4, cols] * second + rows[4:5, cols] * suf[:, cols]
        return begin, adjoint

    def suffix_state(cols):
        other = own_q[:, cols].astype(F32)
        return rows[1:2, cols] * own[:, cols] + rows[2:3, cols] * other, None

    carried(px, pb, pc, pdt, pg, phx, phb, phc, tx, tb, tc, rate, bias, skip, None,
            prompt_state, p_idx, p_idb, p_idc, p_r, p_dx, p_db, p_dc, p_ddt,
            (lx, lb, lc), (ptx, ptb, ptc))
    weight = row_weight(len_ref, adv_ref, mask_ref)
    carried(sx, sb, sc, sdt, sg, shx, shb, shc, tx, tb, tc, rate, bias, skip, weight,
            suffix_state, s_idx, s_idb, s_idc, s_r, s_dx, s_db, s_dc, s_ddt,
            (lx, lb, lc), None)


def remote(src, dst, send, recv, target):
    return pltpu.make_async_remote_copy(
        src_ref=src,
        dst_ref=dst,
        send_sem=send,
        recv_sem=recv,
        device_id={"suf": target},
        device_id_type=MESH,
    )


def greet(ways, me):
    barrier = pltpu.get_barrier_semaphore()
    for d in range(1, ways):
        pl.semaphore_signal(
            barrier, inc=1, device_id={"suf": lax.rem(me + d, ways)}, device_id_type=MESH
        )
    pl.semaphore_wait(barrier, ways - 1)


def halo_kernel(ways, x_ref, out_ref, send, recv):
    me = lax.axis_index("suf")
    last = ways - 1
    greet(ways, me)
    right = remote(x_ref, out_ref.at[0], send.at[last], recv.at[0], lax.rem(me + 1, ways))
    spread = [remote(x_ref, out_ref.at[1], send.at[i], recv.at[1], i) for i in range(last)]

    @pl.when(me < last)
    def _():
        right.start()

    @pl.when(me == last)
    def _():
        for copy in spread:
            copy.start()
        out_ref[1] = x_ref[...]
        for copy in spread:
            copy.wait_send()

    @pl.when(me == 0)
    def _():
        out_ref[0] = jnp.zeros_like(x_ref)

    @pl.when(me < last)
    def _():
        right.wait_send()
        spread[0].wait_recv()

    @pl.when(me > 0)
    def _():
        right.wait_recv()


def halo(block, ways):
    return pl.pallas_call(
        functools.partial(halo_kernel, ways),
        out_shape=jax.ShapeDtypeStruct((2,) + block.shape, block.dtype),
        in_specs=[pl.BlockSpec(memory_space=pltpu.VMEM)],
        out_specs=pl.BlockSpec(memory_space=pltpu.VMEM),
        scratch_shapes=[pltpu.SemaphoreType.DMA((ways,)), pltpu.SemaphoreType.DMA((2,))],
        compiler_params=pltpu.CompilerParams(collective_id=0, has_side_effects=True),
        name="halo",
    )(block)


def sum_kernel(ways, x_ref, out_ref, slots, send, recv):
    me = lax.axis_index("suf")
    last = ways - 1
    greet(ways, me)
    left = remote(x_ref, slots.at[last], send.at[0], recv.at[last], lax.rem(me + last, ways))
    up = remote(x_ref, slots.at[me], send.at[1], recv.at[me], last)

    @pl.when(me > 0)
    def _():
        left.start()

    @pl.when(me < last)
    def _():
        up.start()

    @pl.when(me > 0)
    def _():
        left.wait_send()

    @pl.when(me < last)
    def _():
        up.wait_send()
        left.wait_recv()
        out_ref[0:3] = slots[last][0:3]

    @pl.when(me == last)
    def _():
        total = x_ref[3:6]
        for i in range(last):
            remote(x_ref, slots.at[i], send.at[1], recv.at[i], 0).wait_recv()
            total = total + slots[i][3:6]
        out_ref[0:3] = total


def sum_rows(block, ways):
    return pl.pallas_call(
        functools.partial(sum_kernel, ways),
        out_shape=jax.ShapeDtypeStruct(block.shape, block.dtype),
        in_specs=[pl.BlockSpec(memory_space=pltpu.VMEM)],
        out_specs=pl.BlockSpec(memory_space=pltpu.VMEM),
        scratch_shapes=[
            pltpu.VMEM((ways,) + block.shape, block.dtype),
            pltpu.SemaphoreType.DMA((2,)),
            pltpu.SemaphoreType.DMA((ways,)),
        ],
        compiler_params=pltpu.CompilerParams(collective_id=1, has_side_effects=True),
        name="sum_rows",
    )(block)


def fix_kernel(extra, tx, tb, tc, dx, db, dc, ox, ob, oc):
    at = 0
    row = lax.broadcasted_iota(jnp.int32, (8, 1), 0)
    for tail, source, out in ((tx, dx, ox), (tb, db, ob), (tc, dc, oc)):
        width = tail.shape[1]
        rows = extra[:, at : at + width]
        moved = jnp.concatenate([jnp.zeros((5, width), F32), rows[0:3]], axis=0)
        fixed = tail[...] + jnp.where(row >= 5, moved, 0.0)
        out[...] = jnp.concatenate([source[...].astype(F32)[:8], fixed], axis=0).astype(BF16)
        at += width


def fix(extra, tails, grads):
    full_specs = [pl.BlockSpec(memory_space=pltpu.VMEM)] * 4
    ends = [pl.BlockSpec((16, g.shape[1]), lambda i: (Q // 16 - 1, 0)) for g in grads]
    return pl.pallas_call(
        fix_kernel,
        grid=(1,),
        in_specs=full_specs + ends,
        out_specs=ends,
        out_shape=[jax.ShapeDtypeStruct(g.shape, g.dtype) for g in grads],
        input_output_aliases={4: 0, 5: 1, 6: 2},
        name="fix",
    )(extra, *tails, *grads)


def exchange(parts, bit, ways):
    route = [(i, i ^ bit) for i in range(ways)]
    return [lax.ppermute(part, "suf", route) for part in parts]


def code(value):
    top = jnp.max(jnp.abs(value), axis=0, keepdims=True)
    safe = top > 1e-30
    inverse = jnp.where(safe, 32767.0 / jnp.where(safe, top, 1.0), 0.0)
    return jnp.round(value * inverse).astype(jnp.int16), top * (1.0 / 32767.0)


def combine(own, adj, suf, dec, ways):
    me = lax.axis_index("suf")
    start = jnp.zeros_like(own)
    before = jnp.ones_like(dec)
    tail = jnp.zeros_like(adj)
    after = jnp.ones_like(dec)
    bit = 1
    while bit * 2 < ways:
        upper = (me & bit) != 0
        own_, adj_, suf_, dec_ = exchange((own, adj, suf, dec), bit, ways)
        start = jnp.where(upper, before * own_ + start, start)
        before = jnp.where(upper, before * dec_, before)
        tail = jnp.where(upper, tail, tail + after * adj_)
        after = jnp.where(upper, after, after * dec_)
        own = jnp.where(upper, dec * own_ + own, dec_ * own + own_)
        adj = jnp.where(upper, adj_ + dec_ * adj, adj + dec * adj_)
        suf = suf + suf_
        dec = dec * dec_
        bit *= 2
    upper = (me & bit) != 0
    core = me & 1
    half = own.shape[1] // 2

    def mine(value):
        return jnp.where(core == 0, value[:, :half], value[:, half:])

    second = jnp.where(upper, adj + dec * suf, suf)
    own_q, own_s = code(mine(own))
    sec_q, sec_s = code(mine(second))
    got = exchange((own_q, sec_q, jnp.concatenate([own_s, sec_s, mine(dec)], axis=0)), bit, ways)
    other = exchange(got, 1, ways)

    def whole(a, b):
        return jnp.where(core == 0, jnp.concatenate([a, b], 1), jnp.concatenate([b, a], 1))

    own_q, sec_q, small = [whole(a, b) for a, b in zip(got, other)]
    own_s, sec_s, dec_ = small[0:1], small[1:2], small[2:3]
    zero = jnp.zeros_like(dec)
    rows = [
        jnp.where(upper, before, zero) * own_s,
        jnp.where(upper, jnp.ones_like(dec), dec_),
        jnp.where(upper, dec, jnp.ones_like(dec)) * own_s,
        after * sec_s,
        jnp.where(upper, after, after * dec_),
        zero, zero, zero,
    ]
    return start, own, tail, suf, own_q, sec_q, jnp.concatenate(rows, axis=0)


def shards(
    prefix_x, prefix_b, prefix_c, prefix_dt, prefix_grad,
    suffix_x, suffix_b, suffix_c, suffix_dt, suffix_grad,
    lengths, loss_mask, advantage, conv_x, conv_b, conv_c, decay_rate, dt_bias, skip,
):
    ways = lax.axis_size("suf")
    heads = decay_rate.shape[0]
    groups = conv_b.shape[1] // N
    per = heads // groups
    wide = per * HD
    full = heads * HD
    nb = groups * N

    tails = jnp.concatenate([prefix_x[-16:], prefix_b[-16:], prefix_c[-16:]], axis=1)
    halos = halo(tails, ways)

    def halo_specs(slot):
        def at(width, first):
            return pl.BlockSpec((None, 16, width), lambda g: (slot, 0, first // width + g))

        return [at(wide, 0), at(N, full), at(N, full + nb)]

    sm = pl.BlockSpec(memory_space=pltpu.SMEM)
    sx = pl.BlockSpec((Q, wide), lambda g: (0, g))
    sb = pl.BlockSpec((Q, N), lambda g: (0, g))
    sdt = pl.BlockSpec((per, Q), lambda g: (g, 0))
    hx = pl.BlockSpec((8, wide), lambda g: (0, g))
    hb = pl.BlockSpec((8, N), lambda g: (0, g))
    kx = pl.BlockSpec((KW, wide), lambda g: (0, g))
    kb = pl.BlockSpec((KW, N), lambda g: (0, g))
    ph = pl.BlockSpec((per, 1), lambda g: (g, 0))
    half = [sx, sb, sb, sdt, sx]
    base_specs = (
        [sm, sm, pl.BlockSpec((1, Q), lambda g: (0, 0))] + half + halo_specs(0) + half + halo_specs(1) + [kx, kb, kb, ph, ph, ph]
    )
    base = (
        (lengths, advantage, loss_mask)
        + (prefix_x, prefix_b, prefix_c, prefix_dt, prefix_grad)
        + (halos,) * 3
        + (suffix_x[0], suffix_b[0], suffix_c[0], suffix_dt[:, 0], suffix_grad[0])
        + (halos,) * 3
        + (conv_x, conv_b, conv_c, decay_rate[:, None], dt_bias[:, None], skip[:, None])
    )

    def shape(rows, columns, kind=F32):
        return jax.ShapeDtypeStruct((rows, columns), kind)

    params = pltpu.CompilerParams(vmem_limit_bytes=48 * 1024 * 1024)
    state_shape = shape(N, full)
    own, adj, suf, dec = pl.pallas_call(
        states_kernel,
        grid=(groups,),
        in_specs=base_specs,
        out_specs=[sx, sx, sx, hx],
        out_shape=[state_shape] * 3 + [shape(8, full)],
        compiler_params=params,
        name="states",
    )(*base)

    inner_specs = [sx, sb, sb, sdt]
    inner_shape = [shape(Q, full), shape(Q, nb), shape(Q, nb), shape(heads, Q)]
    inner = pl.pallas_call(
        within_kernel,
        grid=(groups,),
        in_specs=base_specs,
        out_specs=inner_specs * 2,
        out_shape=inner_shape * 2,
        compiler_params=params,
        cost_estimate=pl.CostEstimate(
            flops=heads * 2 * 12 * Q * Q * Q, bytes_accessed=6 << 20, transcendentals=heads * Q * Q
        ),
        name="within",
    )(*base)

    states = combine(own, adj, suf, dec[:1], ways)

    out_specs = [sx, sb, sb, sdt] * 2 + [hx, hb, hb] * 2
    out_shape = [shape(Q, full, BF16), shape(Q, nb, BF16), shape(Q, nb, BF16), shape(heads, Q)] * 2
    out_shape += [shape(8, full), shape(8, nb), shape(8, nb)] * 2
    outs = pl.pallas_call(
        carried_kernel,
        grid=(groups,),
        in_specs=base_specs + [sx] * 6 + [hx] + inner_specs * 2,
        out_specs=out_specs,
        out_shape=out_shape,
        compiler_params=params,
        name="carried",
    )(*base, *states, *inner)

    extra = sum_rows(jnp.concatenate(outs[8:11], axis=1), ways)
    finished = fix(extra, outs[11:14], outs[:3])
    return (
        *finished,
        outs[3],
        outs[4][None],
        outs[5][None],
        outs[6][None],
        outs[7][:, None],
    )


def solution(mesh):
    rows = P(("grp", "suf"), "head")
    deep = P(("grp", "suf"), None, "head")
    flat = P("head", ("grp", "suf"))
    flat3 = P("head", ("grp", "suf"), None)
    one = P(("grp", "suf"))
    return jax.shard_map(
        shards,
        mesh=mesh,
        in_specs=(
            rows, rows, rows, flat, rows,
            deep, deep, deep, flat3, deep,
            one, P(("grp", "suf"), None), one,
            P(None, "head"), P(None, "head"), P(None, "head"),
            P("head"), P("head"), P("head"),
        ),
        out_specs=(rows, rows, rows, flat, deep, deep, deep, flat3),
        check_vma=False,
    )
```

```python
import functools

import jax
import jax.numpy as jnp
from jax import lax
from jax.experimental import pallas as pl
from jax.experimental.pallas import tpu as pltpu
from jax.sharding import PartitionSpec as P

HD = 64
N = 128
KW = 4
Q = 128
F32 = jnp.float32
BF16 = jnp.bfloat16
EXACT = lax.Precision.HIGHEST
MESH = pl.DeviceIdType.MESH
NN = (((1,), (0,)), ((), ()))
NT = (((1,), (1,)), ((), ()))


def mm(a, b, dims=NN):
    return lax.dot_general(a, b, dims, preferred_element_type=F32)


def split(a):
    hi = a.astype(BF16)
    return hi, (a - hi.astype(F32)).astype(BF16)


def mm3(a, b, dims=NN):
    ah, al = a
    bh, bl = b
    axis = dims[0][1][0]
    return mm(
        jnp.concatenate([ah, ah, al], axis=1), jnp.concatenate([bh, bl, bh], axis=axis), dims
    )


def conv_pre(halo, u, taps):
    w = jnp.concatenate([halo.astype(F32)[8:], u.astype(F32)], axis=0)
    taps = taps.astype(F32)
    out = w[5 : 5 + Q] * taps[0:1]
    for k in range(1, KW):
        out = out + w[5 + k : 5 + k + Q] * taps[k : k + 1]
    return out


def silu(v):
    return v * jax.nn.sigmoid(v)


def conv_back(dact, pre, taps):
    taps = taps.astype(F32)
    sig = jax.nn.sigmoid(pre)
    dpre = dact * (sig * (1.0 + pre * (1.0 - sig)))
    zero = jnp.zeros((8, dpre.shape[1]), F32)
    ext = jnp.concatenate([zero, dpre, zero], axis=0)
    du = ext[11 : 11 + Q] * taps[0:1]
    left = ext[8:16] * taps[0:1]
    for k in range(1, KW):
        du = du + ext[11 - k : 11 - k + Q] * taps[k : k + 1]
        left = left + ext[8 - k : 16 - k] * taps[k : k + 1]
    return du, left


def softplus(v):
    return jnp.maximum(v, 0.0) + jnp.log1p(jnp.exp(-jnp.abs(v)))


def tri(transposed=False):
    row = lax.broadcasted_iota(jnp.int32, (Q, Q), 0)
    col = lax.broadcasted_iota(jnp.int32, (Q, Q), 1)
    return (row >= col) if transposed else (row <= col)


def expander(heads):
    row = lax.broadcasted_iota(jnp.int32, (heads, heads * HD), 0)
    col = lax.broadcasted_iota(jnp.int32, (heads, heads * HD), 1)
    return ((col >= row * HD) & (col < (row + 1) * HD)).astype(F32)


def column(row_ref, heads):
    shape = (heads, row_ref.shape[1])
    row = lax.broadcasted_iota(jnp.int32, shape, 0) + pl.program_id(0) * heads
    col = lax.broadcasted_iota(jnp.int32, shape, 1)
    return jnp.sum(jnp.where(row == col, row_ref[...], 0.0), axis=1, keepdims=True)


def decays(dt_ref, bias_ref, rate_ref):
    heads = dt_ref.shape[0]
    rate = column(rate_ref, heads)
    raw = dt_ref[...] + column(bias_ref, heads)
    step = softplus(raw)
    cum = lax.dot_general(
        -step * rate, tri().astype(F32), NN, precision=EXACT, preferred_element_type=F32
    )
    return raw, step, cum


def widen(rows, spread):
    v = rows.T
    hi, rest = split(v)
    lo = (v - hi.astype(F32) - rest.astype(F32)).astype(BF16)
    e = spread.astype(BF16)
    return mm(jnp.concatenate([hi, rest, lo], axis=1), jnp.concatenate([e, e, e], axis=0))


def row_weight(len_ref, adv_ref, mask_ref):
    at = lax.broadcasted_iota(jnp.int32, (1, Q), 1)
    inside = (at < len_ref[0]).astype(F32)
    return adv_ref[0] * mask_ref[...].astype(F32) * inside


def states_kernel(
    len_ref, adv_ref, mask_ref,
    px, pb, pc, pdt, pg, phx, phb, phc,
    sx, sb, sc, sdt, sg, shx, shb, shc,
    tx, tb, tc, rate, bias, skip,
    own_ref, adj_ref, suf_ref, dec_ref,
):
    heads = pdt.shape[0]
    spread = expander(heads)
    raw, step, cum = decays(pdt, bias, rate)
    last = cum[:, Q - 1 : Q]
    push = widen(jnp.exp(last - cum) * step, spread)
    pull = jnp.exp(cum)
    pull_wide = widen(pull, spread)
    dec_ref[...] = jnp.broadcast_to(pull_wide[Q - 1 : Q], dec_ref.shape)
    b_t = split(silu(conv_pre(phb[...], pb[...], tb[...])).T)
    c_t = split(silu(conv_pre(phc[...], pc[...], tc[...])).T)
    x_act = silu(conv_pre(phx[...], px[...], tx[...]))
    own_ref[...] = mm3(b_t, split(x_act * push))
    adj_ref[...] = mm3(c_t, split(pg[...].astype(F32) * pull_wide))
    s_raw, s_step, s_cum = decays(sdt, bias, rate)
    weight = row_weight(len_ref, adv_ref, mask_ref)
    s_pull = widen(jnp.exp(s_cum) * weight, spread)
    sc_t = split(silu(conv_pre(shc[...], sc[...], tc[...])).T)
    suf_ref[...] = mm3(sc_t, split(sg[...].astype(F32) * s_pull))


def within(x_ref, b_ref, c_ref, dt_ref, g_ref, hx, hb, hc, tx, tb, tc, rate, bias, weight,
           dx_out, db_out, dc_out, r_out):
    heads = dt_ref.shape[0]
    raw, step, cum = decays(dt_ref, bias, rate)
    cum_col = cum.T
    step_col = step.T
    b_act = split(silu(conv_pre(hb[...], b_ref[...], tb[...])))
    c_act = split(silu(conv_pre(hc[...], c_ref[...], tc[...])))
    bc = mm3(b_act, c_act, NT)
    keep = tri()
    lane = lax.broadcasted_iota(jnp.int32, (Q, 2 * HD), 1)
    total = jnp.zeros((Q, Q), F32)
    width = heads * HD
    chunk = min(width, 2 * HD)
    for at in range(0, width, chunk):
        cols = slice(at, at + chunk)
        x_act = silu(conv_pre(hx[:, cols], x_ref[:, cols], tx[:, cols]))
        grad = g_ref[:, cols]
        xh, xl = split(x_act)
        twice = jnp.concatenate([grad, grad], axis=1)
        left, right = [], []
        for k in range(chunk // HD):
            h = at // HD + k
            if chunk == HD:
                xhm, xlm, gm = xh, xl, grad
            else:
                mine = (lane >= k * HD) & (lane < (k + 1) * HD)
                zero = jnp.zeros((), BF16)
                xhm = jnp.where(mine, xh, zero)
                xlm = jnp.where(mine, xl, zero)
                gm = jnp.where(mine, grad, zero)
            gap = jnp.where(keep, cum[h : h + 1] - cum_col[:, h : h + 1], -1e30)
            att = jnp.exp(gap) * step_col[:, h : h + 1]
            if weight is not None:
                att = att * weight
            dm = mm(jnp.concatenate([xhm, xlm], axis=1), twice, NT)
            q = dm * att
            total = total + q
            r_out[h : h + 1] = jnp.sum(q * bc, axis=0, keepdims=True)
            mh, ml = split(att * bc)
            left += [mh, ml]
            right += [gm, gm]
        dx_out[:, cols] = mm(jnp.concatenate(left, axis=1), jnp.concatenate(right, axis=0))
    db_out[...] = mm3(split(total), c_act)
    dc_out[...] = mm3(split(total.T), b_act)


def within_kernel(
    len_ref, adv_ref, mask_ref,
    px, pb, pc, pdt, pg, phx, phb, phc,
    sx, sb, sc, sdt, sg, shx, shb, shc,
    tx, tb, tc, rate, bias, skip,
    p_dx, p_db, p_dc, p_r, s_dx, s_db, s_dc, s_r,
):
    within(px, pb, pc, pdt, pg, phx, phb, phc, tx, tb, tc, rate, bias, None, p_dx, p_db, p_dc, p_r)
    weight = row_weight(len_ref, adv_ref, mask_ref)
    within(sx, sb, sc, sdt, sg, shx, shb, shc, tx, tb, tc, rate, bias, weight, s_dx, s_db, s_dc, s_r)


def per_head(value, gather):
    hi, lo = split(value)
    return mm(jnp.concatenate([hi, lo], axis=1), gather)


def carried(x_ref, b_ref, c_ref, dt_ref, g_ref, hx, hb, hc, tx, tb, tc, rate, bias, skip, weight,
            state, in_dx, in_db, in_dc, in_r, dx, db, dc, ddt, lefts, tails):
    heads = dt_ref.shape[0]
    spread = expander(heads)
    raw, step, cum = decays(dt_ref, bias, rate)
    pull = jnp.exp(cum)
    if weight is not None:
        pull = pull * weight
    gain = column(skip, heads)
    if weight is not None:
        gain = gain * weight
    gain = jnp.broadcast_to(gain, (heads, Q))
    last = cum[:, Q - 1 : Q]
    push = jnp.exp(last - cum) * step
    b_pre = conv_pre(hb[...], b_ref[...], tb[...])
    c_pre = conv_pre(hc[...], c_ref[...], tc[...])
    b_act = split(silu(b_pre))
    c_act = split(silu(c_pre))
    dc_act = in_dc[...]
    db_act = in_db[...]
    width = heads * HD
    chunk = min(width, 256)
    across = jnp.zeros((Q, heads), F32)
    col_sum = jnp.zeros((Q, heads), F32)
    v = jnp.zeros((Q, heads), F32)
    both = jnp.zeros((8, heads), F32)
    first = 0 if weight is None else 3
    head_of = lax.broadcasted_iota(jnp.int32, (chunk, heads), 1) * HD
    lane_of = lax.broadcasted_iota(jnp.int32, (chunk, heads), 0)

    def finish(dact, pre, taps, out, left, tail, cols):
        du, dleft = conv_back(dact, pre, taps)
        out[:, cols] = du.astype(BF16)
        left[first : first + 3, cols] = dleft[:3]
        if tail is not None:
            tail[:, cols] = du[Q - 8 :]

    for at in range(0, width, chunk):
        cols = slice(at, at + chunk)
        inside = (lane_of + at >= head_of) & (lane_of + at < head_of + HD)
        gather = inside.astype(BF16)
        gather = jnp.concatenate([gather, gather], axis=0)
        part = spread[:, cols]
        grad = g_ref[:, cols].astype(F32)
        x_pre = conv_pre(hx[:, cols], x_ref[:, cols], tx[:, cols])
        x_act = silu(x_pre)
        start, adjoint = state(cols)
        s_split = split(start)
        pulled = grad * widen(pull, part)
        across = across + per_head(pulled * mm3(c_act, s_split), gather)
        dc_act = dc_act + mm3(split(pulled), s_split, NT)
        dx_in = in_dx[:, cols]
        if adjoint is not None:
            push_wide = widen(push, part)
            a_split = split(adjoint)
            moved = push_wide * mm3(b_act, a_split)
            dx_in = dx_in + moved
            v = v + per_head(x_act * moved, gather)
            db_act = db_act + mm3(split(x_act * push_wide), a_split, NT)
            product = jnp.sum(start * adjoint, axis=0, keepdims=True)
            both = both + per_head(jnp.broadcast_to(product, (8, chunk)), gather)
        col_sum = col_sum + per_head(x_act * dx_in, gather)
        dx_act = dx_in + widen(gain, part) * grad
        finish(dx_act, x_pre, tx[:, cols], dx, lefts[0], tails and tails[0], cols)
    whole = slice(0, N)
    finish(db_act, b_pre, tb[...], db, lefts[1], tails and tails[1], whole)
    finish(dc_act, c_pre, tc[...], dc, lefts[2], tails and tails[2], whole)
    end = jnp.sum(v, axis=0, keepdims=True).T
    if weight is None:
        end = end + jnp.exp(last) * both.T[:, :1]
    cols_t = col_sum.T
    change = in_r[...] + across.T - cols_t
    dlog = end + lax.dot_general(
        change, tri(True).astype(F32), NN, precision=EXACT, preferred_element_type=F32
    )
    ddt[...] = (cols_t / step - column(rate, heads) * dlog) * jax.nn.sigmoid(raw)


def carried_kernel(
    len_ref, adv_ref, mask_ref,
    px, pb, pc, pdt, pg, phx, phb, phc,
    sx, sb, sc, sdt, sg, shx, shb, shc,
    tx, tb, tc, rate, bias, skip,
    start, own, tail, suf, own_got, sec_got, own_other, sec_other, rows,
    p_idx, p_idb, p_idc, p_r, s_idx, s_idb, s_idc, s_r,
    p_dx, p_db, p_dc, p_ddt, s_dx, s_db, s_dc, s_ddt,
    lx, lb, lc, ptx, ptb, ptc,
):
    for left in (lx, lb, lc):
        left[...] = jnp.zeros_like(left)

    def pick(got, other, cols):
        at = cols.start % got.shape[1]
        half = slice(at, at + cols.stop - cols.start)
        here = rows[7:8, cols] > 0.5
        return jnp.where(here, got[:, half].astype(F32), other[:, half].astype(F32))

    def prompt_state(cols):
        other = pick(own_got, own_other, cols)
        second = pick(sec_got, sec_other, cols)
        begin = rows[5:6, cols] * start[:, cols] + rows[0:1, cols] * other
        adjoint = rows[6:7, cols] * tail[:, cols] + rows[3:4, cols] * second
        return begin, adjoint + rows[4:5, cols] * suf[:, cols]

    def suffix_state(cols):
        other = pick(own_got, own_other, cols)
        return rows[1:2, cols] * own[:, cols] + rows[2:3, cols] * other, None

    carried(px, pb, pc, pdt, pg, phx, phb, phc, tx, tb, tc, rate, bias, skip, None,
            prompt_state, p_idx, p_idb, p_idc, p_r, p_dx, p_db, p_dc, p_ddt,
            (lx, lb, lc), (ptx, ptb, ptc))
    weight = row_weight(len_ref, adv_ref, mask_ref)
    carried(sx, sb, sc, sdt, sg, shx, shb, shc, tx, tb, tc, rate, bias, skip, weight,
            suffix_state, s_idx, s_idb, s_idc, s_r, s_dx, s_db, s_dc, s_ddt,
            (lx, lb, lc), None)


def remote(src, dst, send, recv, target):
    return pltpu.make_async_remote_copy(
        src_ref=src,
        dst_ref=dst,
        send_sem=send,
        recv_sem=recv,
        device_id={"suf": target},
        device_id_type=MESH,
    )


def greet(ways, me):
    barrier = pltpu.get_barrier_semaphore()
    for d in range(1, ways):
        pl.semaphore_signal(
            barrier, inc=1, device_id={"suf": lax.rem(me + d, ways)}, device_id_type=MESH
        )
    pl.semaphore_wait(barrier, ways - 1)


def halo_kernel(ways, tx, tb, tc, out_ref, x_ref, send, recv):
    me = lax.axis_index("suf")
    last = ways - 1
    x_ref[...] = jnp.concatenate([tx[...], tb[...], tc[...]], axis=1)
    greet(ways, me)
    right = remote(x_ref, out_ref.at[0], send.at[last], recv.at[0], lax.rem(me + 1, ways))
    spread = [remote(x_ref, out_ref.at[1], send.at[i], recv.at[1], i) for i in range(last)]

    @pl.when(me < last)
    def _():
        right.start()

    @pl.when(me == last)
    def _():
        for copy in spread:
            copy.start()
        out_ref[1] = x_ref[...]
        for copy in spread:
            copy.wait_send()

    @pl.when(me == 0)
    def _():
        out_ref[0] = jnp.zeros_like(x_ref)

    @pl.when(me < last)
    def _():
        right.wait_send()
        spread[0].wait_recv()

    @pl.when(me > 0)
    def _():
        right.wait_recv()


def halo(sources, ways):
    width = sum(source.shape[1] for source in sources)
    return pl.pallas_call(
        functools.partial(halo_kernel, ways),
        grid=(1,),
        out_shape=jax.ShapeDtypeStruct((2, 16, width), BF16),
        in_specs=[
            pl.BlockSpec((16, source.shape[1]), lambda i: (Q // 16 - 1, 0)) for source in sources
        ],
        out_specs=pl.BlockSpec(memory_space=pltpu.VMEM),
        scratch_shapes=[
            pltpu.VMEM((16, width), BF16),
            pltpu.SemaphoreType.DMA((ways,)),
            pltpu.SemaphoreType.DMA((2,)),
        ],
        compiler_params=pltpu.CompilerParams(collective_id=0, has_side_effects=True),
        name="halo",
    )(*sources)


def sum_kernel(ways, lx, lb, lc, out_ref, x_ref, slots, send, recv):
    me = lax.axis_index("suf")
    last = ways - 1
    x_ref[...] = jnp.concatenate([lx[...], lb[...], lc[...]], axis=1)
    greet(ways, me)
    left = remote(x_ref, slots.at[last], send.at[0], recv.at[last], lax.rem(me + last, ways))
    up = remote(x_ref, slots.at[me], send.at[1], recv.at[me], last)

    @pl.when(me > 0)
    def _():
        left.start()

    @pl.when(me < last)
    def _():
        up.start()

    @pl.when(me > 0)
    def _():
        left.wait_send()

    @pl.when(me < last)
    def _():
        up.wait_send()
        left.wait_recv()
        out_ref[0:3] = slots[last][0:3]

    @pl.when(me == last)
    def _():
        total = x_ref[3:6]
        for i in range(last):
            remote(x_ref, slots.at[i], send.at[1], recv.at[i], 0).wait_recv()
            total = total + slots[i][3:6]
        out_ref[0:3] = total


def sum_rows(sources, ways):
    shape = (8, sum(source.shape[1] for source in sources))
    return pl.pallas_call(
        functools.partial(sum_kernel, ways),
        out_shape=jax.ShapeDtypeStruct(shape, F32),
        in_specs=[pl.BlockSpec(memory_space=pltpu.VMEM)] * 3,
        out_specs=pl.BlockSpec(memory_space=pltpu.VMEM),
        scratch_shapes=[
            pltpu.VMEM(shape, F32),
            pltpu.VMEM((ways,) + shape, F32),
            pltpu.SemaphoreType.DMA((2,)),
            pltpu.SemaphoreType.DMA((ways,)),
        ],
        compiler_params=pltpu.CompilerParams(collective_id=1, has_side_effects=True),
        name="sum_rows",
    )(*sources)


def fix_kernel(extra, tx, tb, tc, dx, db, dc, ox, ob, oc):
    at = 0
    row = lax.broadcasted_iota(jnp.int32, (8, 1), 0)
    for tail, source, out in ((tx, dx, ox), (tb, db, ob), (tc, dc, oc)):
        width = tail.shape[1]
        rows = extra[:, at : at + width]
        moved = jnp.concatenate([jnp.zeros((5, width), F32), rows[0:3]], axis=0)
        fixed = tail[...] + jnp.where(row >= 5, moved, 0.0)
        out[...] = jnp.concatenate([source[...].astype(F32)[:8], fixed], axis=0).astype(BF16)
        at += width


def fix(extra, tails, grads):
    full_specs = [pl.BlockSpec(memory_space=pltpu.VMEM)] * 4
    ends = [pl.BlockSpec((16, g.shape[1]), lambda i: (Q // 16 - 1, 0)) for g in grads]
    return pl.pallas_call(
        fix_kernel,
        grid=(1,),
        in_specs=full_specs + ends,
        out_specs=ends,
        out_shape=[jax.ShapeDtypeStruct(g.shape, g.dtype) for g in grads],
        input_output_aliases={4: 0, 5: 1, 6: 2},
        name="fix",
    )(extra, *tails, *grads)


def exchange(parts, bit, ways):
    route = [(i, i ^ bit) for i in range(ways)]
    return [lax.ppermute(part, "suf", route) for part in parts]


def code(value):
    top = jnp.max(jnp.abs(value), axis=0, keepdims=True)
    safe = top > 1e-30
    inverse = jnp.where(safe, 32767.0 / jnp.where(safe, top, 1.0), 0.0)
    return jnp.round(value * inverse).astype(jnp.int16), top * (1.0 / 32767.0)


def combine(own, adj, suf, dec, ways):
    me = lax.axis_index("suf")
    one = jnp.ones_like(dec)
    zero = jnp.zeros_like(dec)
    before, after, start = one, one, None
    bit = 1
    while bit * 2 < ways:
        upper = (me & bit) != 0
        own_, adj_, suf_, dec_ = exchange((own, adj, suf, dec), bit, ways)
        if start is None:
            start, tail = own_, adj_
            start_by, tail_by = jnp.where(upper, one, zero), jnp.where(upper, zero, one)
        else:
            start, tail = start_by * start, tail_by * tail
            start = jnp.where(upper, before * own_ + start, start)
            tail = jnp.where(upper, tail, tail + after * adj_)
            start_by, tail_by = one, one
        before = jnp.where(upper, before * dec_, before)
        after = jnp.where(upper, after, after * dec_)
        own = jnp.where(upper, dec * own_ + own, dec_ * own + own_)
        adj = jnp.where(upper, adj_ + dec_ * adj, adj + dec * adj_)
        suf = suf + suf_
        dec = dec * dec_
        bit *= 2
    upper = (me & bit) != 0
    core = me & 1
    half = own.shape[1] // 2

    def mine(value):
        return jnp.where(core == 0, value[:, :half], value[:, half:])

    second = jnp.where(upper, adj + dec * suf, suf)
    own_q, own_s = code(mine(own))
    sec_q, sec_s = code(mine(second))
    got = exchange((own_q, sec_q, jnp.concatenate([own_s, sec_s, mine(dec)], axis=0)), bit, ways)
    other = exchange(got, 1, ways)

    def whole(a, b):
        return jnp.where(core == 0, jnp.concatenate([a, b], 1), jnp.concatenate([b, a], 1))

    small = whole(got[2], other[2])
    own_s, sec_s, dec_ = small[0:1], small[1:2], small[2:3]
    here = lax.broadcasted_iota(jnp.int32, dec.shape, 1) // half == core
    rows = [
        jnp.where(upper, before, zero) * own_s,
        jnp.where(upper, one, dec_),
        jnp.where(upper, dec, one) * own_s,
        after * sec_s,
        jnp.where(upper, after, after * dec_),
        start_by,
        tail_by,
        here.astype(F32),
    ]
    return start, own, tail, suf, *got[:2], *other[:2], jnp.concatenate(rows, axis=0)


def shards(
    prefix_x, prefix_b, prefix_c, prefix_dt, prefix_grad,
    suffix_x, suffix_b, suffix_c, suffix_dt, suffix_grad,
    lengths, loss_mask, advantage, conv_x, conv_b, conv_c, decay_rate, dt_bias, skip,
):
    ways = lax.axis_size("suf")
    heads = decay_rate.shape[0]
    groups = conv_b.shape[1] // N
    per = heads // groups
    wide = per * HD
    full = heads * HD
    nb = groups * N

    halos = halo((prefix_x, prefix_b, prefix_c), ways)

    def halo_specs(slot):
        def at(width, first):
            return pl.BlockSpec((None, 16, width), lambda g: (slot, 0, first // width + g))

        return [at(wide, 0), at(N, full), at(N, full + nb)]

    sm = pl.BlockSpec(memory_space=pltpu.SMEM)
    sx = pl.BlockSpec((Q, wide), lambda g: (0, g))
    sb = pl.BlockSpec((Q, N), lambda g: (0, g))
    sdt = pl.BlockSpec((per, Q), lambda g: (g, 0))
    hx = pl.BlockSpec((8, wide), lambda g: (0, g))
    hb = pl.BlockSpec((8, N), lambda g: (0, g))
    kx = pl.BlockSpec((KW, wide), lambda g: (0, g))
    kb = pl.BlockSpec((KW, N), lambda g: (0, g))
    ph = pl.BlockSpec((1, heads), lambda g: (0, 0))
    half = [sx, sb, sb, sdt, sx]
    base_specs = (
        [sm, sm, pl.BlockSpec((1, Q), lambda g: (0, 0))] + half + halo_specs(0) + half + halo_specs(1) + [kx, kb, kb, ph, ph, ph]
    )
    base = (
        (lengths, advantage, loss_mask)
        + (prefix_x, prefix_b, prefix_c, prefix_dt, prefix_grad)
        + (halos,) * 3
        + (suffix_x[0], suffix_b[0], suffix_c[0], suffix_dt[:, 0], suffix_grad[0])
        + (halos,) * 3
        + (conv_x, conv_b, conv_c, decay_rate[None], dt_bias[None], skip[None])
    )

    def shape(rows, columns, kind=F32):
        return jax.ShapeDtypeStruct((rows, columns), kind)

    half_width = full // 2
    sq_width = min(wide, half_width)
    sq = pl.BlockSpec((N, sq_width), lambda g: (0, lax.rem(g, half_width // sq_width)))
    params = pltpu.CompilerParams(vmem_limit_bytes=60 * 1024 * 1024)
    state_shape = shape(N, full)
    own, adj, suf, dec = pl.pallas_call(
        states_kernel,
        grid=(groups,),
        in_specs=base_specs,
        out_specs=[sx, sx, sx, hx],
        out_shape=[state_shape] * 3 + [shape(8, full)],
        compiler_params=params,
        name="states",
    )(*base)

    inner_specs = [sx, sb, sb, sdt]
    inner_shape = [shape(Q, full), shape(Q, nb), shape(Q, nb), shape(heads, Q)]
    inner = pl.pallas_call(
        within_kernel,
        grid=(groups,),
        in_specs=base_specs,
        out_specs=inner_specs * 2,
        out_shape=inner_shape * 2,
        compiler_params=params,
        cost_estimate=pl.CostEstimate(
            flops=heads * 2 * 12 * Q * Q * Q, bytes_accessed=6 << 20, transcendentals=heads * Q * Q
        ),
        name="within",
    )(*base)

    states = combine(own, adj, suf, dec[:1], ways)

    out_specs = [sx, sb, sb, sdt] * 2 + [hx, hb, hb] * 2
    out_shape = [shape(Q, full, BF16), shape(Q, nb, BF16), shape(Q, nb, BF16), shape(heads, Q)] * 2
    out_shape += [shape(8, full), shape(8, nb), shape(8, nb)] * 2
    outs = pl.pallas_call(
        carried_kernel,
        grid=(groups,),
        in_specs=base_specs + [sx] * 4 + [sq] * 4 + [hx] + inner_specs * 2,
        out_specs=out_specs,
        out_shape=out_shape,
        compiler_params=params,
        name="carried",
    )(*base, *states, *inner)

    extra = sum_rows(outs[8:11], ways)
    finished = fix(extra, outs[11:14], outs[:3])
    return (
        *finished,
        outs[3],
        outs[4][None],
        outs[5][None],
        outs[6][None],
        outs[7][:, None],
    )


def solution(mesh):
    rows = P(("grp", "suf"), "head")
    deep = P(("grp", "suf"), None, "head")
    flat = P("head", ("grp", "suf"))
    flat3 = P("head", ("grp", "suf"), None)
    one = P(("grp", "suf"))
    return jax.shard_map(
        shards,
        mesh=mesh,
        in_specs=(
            rows, rows, rows, flat, rows,
            deep, deep, deep, flat3, deep,
            one, P(("grp", "suf"), None), one,
            P(None, "head"), P(None, "head"), P(None, "head"),
            P("head"), P("head"), P("head"),
        ),
        out_specs=(rows, rows, rows, flat, deep, deep, deep, flat3),
        check_vma=False,
    )
```
